512 devices in a mesh: tour: 128 (over z, y_lo, x, core), width: 4 (over y_hi).
Axes of the slice: x: 4, y: 8 (y_hi: 4, y_lo: 2; y = y_hi * 2 + y_lo), z: 8, core: 2. Of those that a mesh axis runs over, the one named last changes fastest.
Arguments:
- images: bfloat16 [32768, 1152], P('tour', 'width'), may hold values from -1.1953125 to 1.1953125
- texts: bfloat16 [32768, 1152], P('tour', 'width'), may hold values from -1.1953125 to 1.1953125
- matches: int32 [128, 256], P('tour'), may hold values from 0 to 255, each once within a row
- scale: float32 [1], replicated, may hold values from 0.7 to 2.5
- shift_bias: float32 [1], replicated, may hold values from -3 to 0
Outputs:
- grad_images: float32 [32768, 1152], P('tour', 'width')
- grad_texts: float32 [32768, 1152], P('tour', 'width')
The draws below stay inside these ranges and needn't reach their ends.
All inputs are finite; a program needn't handle non-finite values.
Results may differ from the reference program's by a relative error of at most 0.0025.
Values may be sent and summed in bfloat16 or wider, within the bound.
No kernel may reach another device: no remote copies, remote signals or barrier semaphores. Data moves between devices by JAX's collectives and lax.ppermute only.
A program may use at most 64 MiB of HBM per device.

```python
import math
import jax
import jax.numpy as jnp
from jax import lax

D = 1152
B = 256
REACH = 7
BLOCKS = 128
ROWS = 32768


def block_levels(stream_key, dims, shards, smallest, high):
    gain, own = 1.0, jax.random.fold_in(stream_key, 6)
    for axis_at, shards_of in shards:
        draws = jnp.exp(jax.random.uniform(jax.random.fold_in(own, axis_at), (shards_of,), jnp.float32, smallest / len(shards), high / len(shards)))
        gain = gain * jnp.repeat(draws, dims[axis_at] // shards_of).reshape([-1 if axis == axis_at else 1 for axis in range(len(dims))])
    return gain


def scatter_about(key, dims, width, most, split=(), kind=jnp.bfloat16):
    values = jax.random.normal(key, dims, jnp.float32) * width
    if len(split) > 0:
        values = block_levels(key, dims, split, -0.22, 0.18) * values
    return jnp.clip(values, min=-most, max=most).astype(kind)


def setup_inputs(seed: int = 0) -> dict:
    seeds = jax.random.split(jax.random.key(seed), 6)
    images = scatter_about(seeds[0], (ROWS, D), 0.17, 1.1953125, ((0, 128), (1, 4)))
    texts = scatter_about(seeds[1], (ROWS, D), 0.17, 1.1953125, ((0, 128), (1, 4)))
    matches = jax.vmap(lambda own: jax.random.permutation(own, B))(jax.random.split(seeds[2], BLOCKS)).reshape((BLOCKS, B)).astype(jnp.int32)
    scale = jnp.clip(jnp.exp(jax.random.uniform(seeds[3], (1,), jnp.float32, math.log(0.7), math.log(2.5))), 0.7, 2.5)
    shift_bias = jnp.clip(jax.random.uniform(seeds[4], (1,), jnp.float32, -3.0, 0.0), -3.0, 0.0)
    return dict(images=images, texts=texts, matches=matches, scale=scale, shift_bias=shift_bias)


def reference(images, texts, matches, scale, shift_bias):
    temper = scale[0]
    offset_bias = shift_bias[0]
    image_blocks = images.reshape(BLOCKS, B, D).astype(jnp.float32)
    text_blocks = texts.reshape(BLOCKS, B, D).astype(jnp.float32)
    columns = jnp.arange(B, dtype=jnp.int32)
    positive = (matches[:, :, None] == columns[None, None, :]).astype(jnp.float32)
    grad_image = jnp.zeros((BLOCKS, B, D), jnp.float32)
    grad_text = jnp.zeros((BLOCKS, B, D), jnp.float32)
    for offset in range(-REACH, REACH + 1):
        other = jnp.roll(text_blocks, offset, axis=0)
        logits = temper * jnp.einsum("nad,ncd->nac", image_blocks, other) + offset_bias
        probs = jax.nn.sigmoid(logits)
        if offset == 0:
            probs = probs - positive
        weights = lax.optimization_barrier(probs.astype(jnp.bfloat16)).astype(jnp.float32)
        grad_image = grad_image + jnp.einsum("nac,ncd->nad", weights, other)
        grad_text = grad_text + jnp.roll(jnp.einsum("nac,nad->ncd", weights, image_blocks), -offset, axis=0)
    return (temper * grad_image).reshape(ROWS, D), (temper * grad_text).reshape(ROWS, D)
```

```python
import jax
import jax.numpy as jnp
from jax import lax
from jax.sharding import Mesh, PartitionSpec as P

CORES = 2
WIDTH = 4
NEAR = 3


def from_chip(block, distance):
    chips = lax.axis_size("chip")
    route = [((i + distance) % chips, i) for i in range(chips)]
    return lax.ppermute(block, "chip", route)


def from_far_chip(block):
    chips = lax.axis_size("chip")
    route = []
    for i in range(chips):
        for w in range(WIDTH):
            source = (i + (NEAR + 1 if w < WIDTH // 2 else -NEAR - 1)) % chips
            route.append((source * WIDTH + w, i * WIDTH + w))
    return lax.ppermute(block, ("chip", "width"), route)


def swap_cores(block):
    return lax.ppermute(block, "core", [(0, 1), (1, 0)])


def from_width(block, distance):
    route = [((i + distance) % WIDTH, i) for i in range(WIDTH)]
    return lax.ppermute(block, "width", route)


def gather_width(block):
    rows = block.shape[0]
    w = lax.axis_index("width")
    parts = [block] + [from_width(block, d) for d in (1, -1, 2)]
    order = [0, 1, 3, 2]
    return parts


def per_device(images, texts, matches, scale, shift_bias):
    temper = scale[0]
    offset_bias = shift_bias[0]
    first = lax.axis_index("core") == 0
    w = lax.axis_index("width")
    features, rows = images.shape[1], images.shape[0]
    quarter = CORES * rows // WIDTH

    image, text = images.T, texts.T
    marks = jnp.pad(matches.astype(jnp.bfloat16), ((0, 15), (0, rows)))
    mine = jnp.concatenate([jnp.concatenate([image, text], 1), marks], 0)
    other = swap_cores(mine)
    other_image, other_text = other[:features, :rows], other[:features, rows:]
    other_matches = other[features : features + 1, :rows].astype(jnp.int32)

    part0 = jnp.where(first, image, other_text)
    part1 = jnp.where(first, other_image, text)
    full = jnp.concatenate(
        [jnp.where(first, text, other_image), jnp.where(first, other_text, image)], 1
    )
    chunks = jnp.stack(
        [part0[:, :quarter], part0[:, quarter:], part1[:, :quarter], part1[:, quarter:]]
    )
    own = lax.all_to_all(chunks, "width", 0, 0).reshape(WIDTH * features, quarter)

    pieces = [own]
    for step in range(1, NEAR + 1):
        pieces += [from_chip(own, step), from_chip(own, -step)]
    pieces.append(from_far_chip(own))
    held = lax.all_gather(full, "width", axis=0, tiled=True)

    both = jnp.concatenate(
        [jnp.where(first, matches, other_matches), jnp.where(first, other_matches, matches)], 1
    )
    lane = lax.broadcasted_iota(jnp.int32, (1, CORES * rows), 1)
    sub = lax.broadcasted_iota(jnp.int32, (quarter, 1), 0)
    block_of = w // CORES
    goal = jnp.where(first, lane % rows, both)
    goal = jnp.where(lane // rows == block_of, goal, -1)
    mark = lax.dynamic_slice(both, (0, w * quarter), (1, quarter)).reshape(quarter, 1)
    have = jnp.where(first, mark, sub + (w % CORES) * quarter)
    label = (goal == have).astype(jnp.float32)
    kept = (lane // rows != block_of).astype(jnp.float32)

    table = jnp.concatenate(pieces, 1)
    logits = lax.dot_general(
        table, held, (((0,), (0,)), ((), ())), preferred_element_type=jnp.float32
    )
    probs = jax.nn.sigmoid(temper * logits + offset_bias)
    n = table.shape[1]
    probs = jnp.concatenate(
        [probs[:quarter] - label, probs[quarter : n - quarter], probs[n - quarter :] * kept], 0
    )
    weights = probs.astype(jnp.bfloat16)
    partial = jnp.dot(table, weights, preferred_element_type=jnp.float32).astype(jnp.bfloat16)
    partial = partial.reshape(WIDTH, features, CORES, rows).transpose(2, 0, 1, 3)
    partial = partial.reshape(CORES * WIDTH, features, rows)
    terms = lax.all_to_all(partial, ("core", "width"), 0, 0).astype(jnp.float32)
    grad_text = terms[0] + terms[1] + terms[2] + terms[3]
    grad_image = terms[4] + terms[5] + terms[6] + terms[7]
    return (temper * grad_image).T, (temper * grad_text).T


def solution(mesh):
    chips = mesh.shape["tour"] // CORES
    fine = Mesh(mesh.devices.reshape(chips, CORES, WIDTH), ("chip", "core", "width"))
    rows, split = ("chip", "core"), "width"
    return jax.shard_map(
        per_device,
        mesh=fine,
        in_specs=(P(rows, split), P(rows, split), P(rows, None), P(), P()),
        out_specs=(P(rows, split), P(rows, split)),
        check_vma=False,
    )
```

```python
import jax
import jax.numpy as jnp
from jax import lax
from jax.experimental import pallas as pl
from jax.experimental.pallas import tpu as pltpu
from jax.sharding import Mesh, PartitionSpec as P

CORES = 2
WIDTH = 4
LEVELS = 2
LINE = 4
BF16 = jnp.bfloat16
F32 = jnp.float32
SMEM = pl.BlockSpec(memory_space=pltpu.SMEM)
HBM = pl.BlockSpec(memory_space=pl.ANY)
LOCAL = pl.BlockSpec(memory_space=pltpu.VMEM)
PIECES = 2 * LINE
MARKS = 16


def swap_cores(block):
    return lax.ppermute(block, "core", [(0, 1), (1, 0)])


def along_line(block, distance):
    return lax.ppermute(block, "x", [((i + distance) % LINE, i) for i in range(LINE)])


def far_route(rows):
    route = []
    for i in range(rows):
        route += [(2 * i, 2 * ((i + 1) % rows)), (2 * i + 1, 2 * ((i - 1) % rows) + 1)]
    return route


def pack_kernel(image, text, matches, out):
    features, rows = image.shape
    out[:features, :rows] = image[...]
    out[:features, rows:] = text[...]
    marks = jnp.broadcast_to(matches[...], (MARKS, rows)).astype(F32).astype(BF16)
    out[features:, :rows] = marks
    out[features:, rows:] = marks


def deal_kernel(mine, other, chunks, full):
    rows = full.shape[1] // CORES
    features = full.shape[0]
    n = chunks.shape[2]
    first = lax.axis_index("core") == 0
    image, text = mine[:features, :rows], mine[:features, rows:]
    other_image, other_text = other[:features, :rows], other[:features, rows:]
    parts = (
        jnp.where(first, image, other_text),
        jnp.where(first, other_image, text),
    )
    for i in range(LEVELS * WIDTH):
        q = i % WIDTH
        chunks[i] = parts[q // 2][:, (q % 2) * n : (q % 2 + 1) * n]
    full[:, :rows] = jnp.where(first, text, other_image)
    full[:, rows:] = jnp.where(first, other_text, image)


def core_kernel(scalars, have, goal, dealt, far, l1, l2, l3, h1, h2, h3, held, out, pieces, sems):
    span = held.shape[1]
    whole, n = l1.shape
    rows = span // CORES
    features = whole // WIDTH
    w, level = lax.axis_index("width"), lax.axis_index("level")
    block = w // 2
    from_pair = (w < 2) == (level == 0)

    def put(source, p):
        return pltpu.make_async_copy(source, pieces.at[:, pl.ds(p * n, n)], sems.at[p])

    copies = [put(part, p) for p, part in enumerate((dealt.at[level], l1, l2, l3, h1, h2, h3))]
    for copy in copies:
        copy.start()

    @pl.when(from_pair)
    def _():
        last = put(dealt.at[1 - level], PIECES - 1)
        last.start()
        last.wait()

    @pl.when(jnp.logical_not(from_pair))
    def _():
        last = put(far, PIECES - 1)
        last.start()
        last.wait()

    for copy in copies:
        copy.wait()
    logits = lax.dot_general(
        pieces[...], held[...], (((0,), (0,)), ((), ())), preferred_element_type=F32
    )
    probs = jax.nn.sigmoid(scalars[0] * logits + scalars[1])
    label = (have[...] == goal[...]).astype(F32)
    lane = lax.broadcasted_iota(jnp.int32, (n, span), 1)
    last = probs.shape[0] - n
    weights = jnp.concatenate(
        [
            (probs[:n] - label).astype(BF16),
            probs[n:last].astype(BF16),
            jnp.where(lane // rows != block, probs[last:], 0.0).astype(BF16),
        ],
        0,
    )
    for to in range(WIDTH):
        total = jnp.dot(
            pieces[to * features : (to + 1) * features, :], weights, preferred_element_type=F32
        ).astype(BF16)
        for core in range(CORES):
            out[core * WIDTH + to] = total[:, core * rows : (core + 1) * rows]


def per_device(images, texts, matches, scale, shift_bias):
    first = lax.axis_index("core") == 0
    w = lax.axis_index("width")
    x = lax.axis_index("x")
    level = lax.axis_index("level")
    features, rows = images.shape[1], images.shape[0]
    span = CORES * rows
    quarter = span // WIDTH
    whole = WIDTH * features
    block = w // 2
    scalars = jnp.concatenate([scale, shift_bias])

    image, text = images.T, texts.T
    mine = pl.pallas_call(
        pack_kernel,
        out_shape=jax.ShapeDtypeStruct((features + MARKS, CORES * rows), BF16),
        in_specs=[LOCAL] * 3,
        out_specs=LOCAL,
        compiler_params=pltpu.CompilerParams(vmem_limit_bytes=6 << 20),
    )(image, text, matches)
    other = swap_cores(mine)
    other_matches = other[features : features + 1, :rows].astype(jnp.int32)
    chunks, full = pl.pallas_call(
        deal_kernel,
        out_shape=[
            jax.ShapeDtypeStruct((LEVELS * WIDTH, features, quarter), BF16),
            jax.ShapeDtypeStruct((features, span), BF16),
        ],
        in_specs=[LOCAL] * 2,
        out_specs=[LOCAL] * 2,
        compiler_params=pltpu.CompilerParams(vmem_limit_bytes=6 << 20),
    )(mine, other)
    dealt = lax.all_to_all(chunks, ("level", "width"), 0, 0).reshape(LEVELS, whole, quarter)
    own = lax.dynamic_index_in_dim(dealt, level, 0, False)
    pair = lax.dynamic_index_in_dim(dealt, 1 - level, 0, False)

    held = lax.all_to_all(jnp.broadcast_to(full[None], (WIDTH,) + full.shape), "width", 0, 0)
    held = held.reshape(whole, span)
    far = lax.ppermute(pair, ("row", "level"), far_route(lax.axis_size("row")))
    l1, l2, l3 = (along_line(own, d) for d in (1, 2, 3))

    def to_send(d):
        higher = (x + d) % LINE > x
        return jnp.where(higher == (level == 0), pair, far)

    h1, h2, h3 = (along_line(to_send(LINE - d), d) for d in (1, 2, 3))

    both = jnp.concatenate(
        [jnp.where(first, matches, other_matches), jnp.where(first, other_matches, matches)], 1
    )
    lane = lax.broadcasted_iota(jnp.int32, (1, span), 1)
    sub = lax.broadcasted_iota(jnp.int32, (quarter, 1), 0)
    goal = jnp.where(first, lane % rows, both)
    goal = jnp.where(lane // rows == block, goal, -1)
    mark = lax.dynamic_slice(both, (0, w * quarter), (1, quarter)).reshape(quarter, 1)
    have = jnp.where(first, mark, sub + (w % CORES) * quarter)

    partial = pl.pallas_call(
        core_kernel,
        out_shape=jax.ShapeDtypeStruct((CORES * WIDTH, features, rows), BF16),
        in_specs=[SMEM, LOCAL, LOCAL] + [LOCAL] * 9,
        out_specs=LOCAL,
        scratch_shapes=[
            pltpu.VMEM((whole, PIECES * quarter), BF16),
            pltpu.SemaphoreType.DMA((PIECES,)),
        ],
        compiler_params=pltpu.CompilerParams(vmem_limit_bytes=14 << 20),
        cost_estimate=pl.CostEstimate(
            flops=4 * whole * PIECES * quarter * span, bytes_accessed=6 << 20, transcendentals=0
        ),
    )(scalars, have, goal, dealt, far, l1, l2, l3, h1, h2, h3, held)
    terms = lax.all_to_all(partial, ("core", "width"), 0, 0).astype(F32)
    grad_text = terms[0] + terms[1] + terms[2] + terms[3]
    grad_image = terms[4] + terms[5] + terms[6] + terms[7]
    return (scale[0] * grad_image).T, (scale[0] * grad_text).T


def solution(mesh):
    deep = mesh.shape["tour"] // (LEVELS * LINE * CORES)
    fine = Mesh(
        mesh.devices.reshape(deep, LEVELS, LINE, CORES, WIDTH),
        ("row", "level", "x", "core", "width"),
    )
    rows, split = ("row", "level", "x", "core"), "width"
    return jax.shard_map(
        per_device,
        mesh=fine,
        in_specs=(P(rows, split), P(rows, split), P(rows, None), P(), P()),
        out_specs=(P(rows, split), P(rows, split)),
        check_vma=False,
    )
```

```python
import jax
import jax.numpy as jnp
from jax import lax
from jax.experimental import pallas as pl
from jax.experimental.pallas import tpu as pltpu
from jax.sharding import Mesh, PartitionSpec as P

CORES = 2
WIDTH = 4
LEVELS = 2
LINE = 4
BF16 = jnp.bfloat16
F32 = jnp.float32
SMEM = pl.BlockSpec(memory_space=pltpu.SMEM)
HBM = pl.BlockSpec(memory_space=pltpu.HBM)
LOCAL = pl.BlockSpec(memory_space=pltpu.VMEM)
PIECES = 2 * LINE
MARKS = 16


def swap_cores(block):
    return lax.ppermute(block, "core", [(0, 1), (1, 0)])


def along_line(block, distance):
    return lax.ppermute(block, "x", [((i + distance) % LINE, i) for i in range(LINE)])


def far_route(rows):
    route = []
    for i in range(rows):
        route += [(2 * i, 2 * ((i + 1) % rows)), (2 * i + 1, 2 * ((i - 1) % rows) + 1)]
    return route


def pack_kernel(image, text, matches, out, sems):
    features, rows = image.shape
    copies = [
        pltpu.make_async_copy(
            source, out.at[pl.ds(0, features), pl.ds(i * rows, rows)], sems.at[i]
        )
        for i, source in enumerate((image, text))
    ]
    for copy in copies:
        copy.start()
    marks = jnp.broadcast_to(matches[...], (MARKS, rows)).astype(F32).astype(BF16)
    out[features:, :rows] = marks
    out[features:, rows:] = marks
    for copy in copies:
        copy.wait()


def deal_kernel(mine, other, chunks, spread, marks):
    rows = spread.shape[2] // CORES
    features = spread.shape[1]
    n = chunks.shape[2]
    first = lax.axis_index("core") == 0
    image, text = mine[:features, :rows], mine[:features, rows:]
    other_image, other_text = other[:features, :rows], other[:features, rows:]
    parts = (
        jnp.where(first, image, other_text),
        jnp.where(first, other_image, text),
    )
    for i in range(LEVELS * WIDTH):
        q = i % WIDTH
        chunks[i] = parts[q // 2][:, (q % 2) * n : (q % 2 + 1) * n]
    own_marks, other_marks = mine[features:, :rows].astype(F32), other[features:, :rows].astype(F32)
    marks[:, :rows] = jnp.where(first, own_marks, other_marks)
    marks[:, rows:] = jnp.where(first, other_marks, own_marks)
    full = (jnp.where(first, text, other_image), jnp.where(first, other_text, image))
    for i in range(WIDTH):
        spread[i, :, :rows] = full[0]
        spread[i, :, rows:] = full[1]


def weighed(pieces, held, scale, bias):
    logits = lax.dot_general(
        pieces, held[...], (((0,), (0,)), ((), ())), preferred_element_type=F32
    )
    return jax.nn.sigmoid(scale[0] * logits + bias[0])


def label_of(marks, n):
    span = marks.shape[1]
    rows = span // CORES
    first, w = lax.axis_index("core") == 0, lax.axis_index("width")
    mark = marks[0:1, pl.ds(pl.multiple_of(w * n, n), n)]
    down = lax.broadcasted_iota(jnp.int32, (n, n), 0)
    across = lax.broadcasted_iota(jnp.int32, (n, n), 1)
    mark = jnp.sum(jnp.where(down == across, mark, 0.0), axis=1, keepdims=True)
    row = lax.broadcasted_iota(jnp.int32, (n, 1), 0) + lax.rem(w, CORES) * n
    have = jnp.where(first, mark, row.astype(F32))
    lane = lax.broadcasted_iota(jnp.int32, (1, span), 1)
    goal = jnp.where(first, (lane % rows).astype(F32), marks[0:1, :])
    goal = jnp.where(lane // rows == w // CORES, goal, -1.0)
    return (have == goal).astype(F32)


def near_kernel(scale, bias, marks, dealt, l1, l2, l3, held, out):
    n = l1.shape[1]
    own = dealt[lax.axis_index("level")]
    pieces = jnp.concatenate([own, l1[...], l2[...], l3[...]], 1)
    probs = weighed(pieces, held, scale, bias)
    weights = jnp.concatenate([(probs[:n] - label_of(marks, n)).astype(BF16), probs[n:].astype(BF16)], 0)
    out[...] = jnp.dot(pieces, weights, preferred_element_type=F32)


def far_kernel(scale, bias, dealt, far, h1, h2, h3, held, near, out):
    whole, n = h1.shape
    span = held.shape[1]
    rows = span // CORES
    features = whole // WIDTH
    w, level = lax.axis_index("width"), lax.axis_index("level")
    last = jnp.where((w < 2) == (level == 0), dealt[1 - level], far[...])
    pieces = jnp.concatenate([last, h1[...], h2[...], h3[...]], 1)
    probs = weighed(pieces, held, scale, bias)
    lane = lax.broadcasted_iota(jnp.int32, (n, span), 1)
    weights = jnp.concatenate(
        [
            jnp.where(lane // rows != w // 2, probs[:n], 0.0).astype(BF16),
            probs[n:].astype(BF16),
        ],
        0,
    )
    for to in range(WIDTH):
        at = slice(to * features, (to + 1) * features)
        total = near[at, :] + jnp.dot(pieces[at], weights, preferred_element_type=F32)
        total = total.astype(BF16)
        for core in range(CORES):
            out[core * WIDTH + to] = total[:, core * rows : (core + 1) * rows]


def per_device(images, texts, matches, scale, shift_bias):
    x = lax.axis_index("x")
    level = lax.axis_index("level")
    features, rows = images.shape[1], images.shape[0]
    span = CORES * rows
    quarter = span // WIDTH
    whole = WIDTH * features

    image, text = images.T, texts.T
    mine = pl.pallas_call(
        pack_kernel,
        out_shape=jax.ShapeDtypeStruct((features + MARKS, CORES * rows), BF16),
        in_specs=[HBM, HBM, LOCAL],
        out_specs=LOCAL,
        scratch_shapes=[pltpu.SemaphoreType.DMA((2,))],
        compiler_params=pltpu.CompilerParams(vmem_limit_bytes=6 << 20),
    )(image, text, matches)
    other = swap_cores(mine)
    chunks, spread, marks = pl.pallas_call(
        deal_kernel,
        out_shape=[
            jax.ShapeDtypeStruct((LEVELS * WIDTH, features, quarter), BF16),
            jax.ShapeDtypeStruct((WIDTH, features, span), BF16),
            jax.ShapeDtypeStruct((MARKS, span), F32),
        ],
        in_specs=[LOCAL] * 2,
        out_specs=[LOCAL] * 3,
        compiler_params=pltpu.CompilerParams(vmem_limit_bytes=6 << 20),
    )(mine, other)
    dealt = lax.all_to_all(chunks, ("level", "width"), 0, 0).reshape(LEVELS, whole, quarter)
    own = lax.dynamic_index_in_dim(dealt, level, 0, False)
    pair = lax.dynamic_index_in_dim(dealt, 1 - level, 0, False)

    held = lax.all_to_all(spread, "width", 0, 0)
    held = held.reshape(whole, span)
    far = lax.ppermute(pair, ("row", "level"), far_route(lax.axis_size("row")))
    l1, l2, l3 = (along_line(own, d) for d in (1, 2, 3))

    def to_send(d):
        higher = (x + d) % LINE > x
        return jnp.where(higher == (level == 0), pair, far)

    h1, h2, h3 = (along_line(to_send(LINE - d), d) for d in (1, 2, 3))

    cost = pl.CostEstimate(
        flops=2 * whole * PIECES * quarter * span, bytes_accessed=5 << 20, transcendentals=0
    )
    params = pltpu.CompilerParams(vmem_limit_bytes=12 << 20)
    near = pl.pallas_call(
        near_kernel,
        out_shape=jax.ShapeDtypeStruct((whole, span), F32),
        in_specs=[SMEM, SMEM] + [LOCAL] * 6,
        out_specs=LOCAL,
        compiler_params=params,
        cost_estimate=cost,
    )(scale, shift_bias, marks, dealt, l1, l2, l3, held)
    partial = pl.pallas_call(
        far_kernel,
        out_shape=jax.ShapeDtypeStruct((CORES * WIDTH, features, rows), BF16),
        in_specs=[SMEM, SMEM] + [LOCAL] * 7,
        out_specs=LOCAL,
        compiler_params=params,
        cost_estimate=cost,
    )(scale, shift_bias, dealt, far, h1, h2, h3, held, near)
    terms = lax.all_to_all(partial, ("core", "width"), 0, 0).astype(F32)
    grad_text = terms[0] + terms[1] + terms[2] + terms[3]
    grad_image = terms[4] + terms[5] + terms[6] + terms[7]
    return (scale[0] * grad_image).T, (scale[0] * grad_text).T


def solution(mesh):
    deep = mesh.shape["tour"] // (LEVELS * LINE * CORES)
    fine = Mesh(
        mesh.devices.reshape(deep, LEVELS, LINE, CORES, WIDTH),
        ("row", "level", "x", "core", "width"),
    )
    rows, split = ("row", "level", "x", "core"), "width"
    return jax.shard_map(
        per_device,
        mesh=fine,
        in_specs=(P(rows, split), P(rows, split), P(rows, None), P(), P()),
        out_specs=(P(rows, split), P(rows, split)),
        check_vma=False,
    )
```

```python
import jax
import jax.numpy as jnp
from jax import lax
from jax.experimental import pallas as pl
from jax.experimental.pallas import tpu as pltpu
from jax.sharding import Mesh, PartitionSpec as P

CORES = 2
WIDTH = 4
LEVELS = 2
LINE = 4
BF16 = jnp.bfloat16
F32 = jnp.float32
SMEM = pl.BlockSpec(memory_space=pltpu.SMEM)
LOCAL = pl.BlockSpec(memory_space=pltpu.VMEM)
PIECES = 2 * LINE
MARKS = 16


def swap_cores(block):
    return lax.ppermute(block, "core", [(0, 1), (1, 0)])


def along_line(block, distance):
    return lax.ppermute(block, "x", [((i + distance) % LINE, i) for i in range(LINE)])


def far_route(rows):
    route = []
    for i in range(rows):
        route += [(2 * i, 2 * ((i + 1) % rows)), (2 * i + 1, 2 * ((i - 1) % rows) + 1)]
    return route


def deal_kernel(mine, other, chunks):
    n = chunks.shape[2]
    first = lax.axis_index("core") == 0
    parts = (
        jnp.where(first, mine[...], other[...]),
        jnp.where(first, other[...], mine[...]),
    )
    for i in range(LEVELS * WIDTH):
        q = i % WIDTH
        chunks[i] = parts[q // 2][:, (q % 2) * n : (q % 2 + 1) * n]


def spread_kernel(mine, matches, other, spread, marks):
    features, rows = mine.shape
    first = lax.axis_index("core") == 0
    own, others = mine[...], other[:features, :]
    full = (jnp.where(first, own, others), jnp.where(first, others, own))
    for i in range(WIDTH):
        spread[i, :, :rows] = full[0]
        spread[i, :, rows:] = full[1]
    own_marks = jnp.broadcast_to(matches[...].astype(F32), (MARKS, rows))
    other_marks = other[features:, :].astype(F32)
    marks[:, :rows] = jnp.where(first, own_marks, other_marks)
    marks[:, rows:] = jnp.where(first, other_marks, own_marks)


def weighed(pieces, held, scale, bias):
    logits = lax.dot_general(
        pieces, held[...], (((0,), (0,)), ((), ())), preferred_element_type=F32
    )
    return jax.nn.sigmoid(scale[0] * logits + bias[0])


def halo_kernel(pair, far, *outs):
    x, level = lax.axis_index("x"), lax.axis_index("level")
    for d, out in enumerate(outs, 1):
        higher = lax.rem(x + d, LINE) > x
        out[...] = jnp.where(higher == (level == 0), pair[...], far[...])


def label_of(marks, n):
    span = marks.shape[1]
    rows = span // CORES
    first, w = lax.axis_index("core") == 0, lax.axis_index("width")
    mark = marks[0:1, pl.ds(pl.multiple_of(w * n, n), n)]
    down = lax.broadcasted_iota(jnp.int32, (n, n), 0)
    across = lax.broadcasted_iota(jnp.int32, (n, n), 1)
    mark = jnp.sum(jnp.where(down == across, mark, 0.0), axis=1, keepdims=True)
    row = lax.broadcasted_iota(jnp.int32, (n, 1), 0) + lax.rem(w, CORES) * n
    have = jnp.where(first, mark, row.astype(F32))
    lane = lax.broadcasted_iota(jnp.int32, (1, span), 1)
    goal = jnp.where(first, (lane % rows).astype(F32), marks[0:1, :])
    goal = jnp.where(lane // rows == w // CORES, goal, -1.0)
    return (have == goal).astype(F32)


def near_kernel(scale, bias, marks, dealt, l1, l2, l3, held, out):
    n = l1.shape[1]
    own = dealt[lax.axis_index("level")]
    pieces = jnp.concatenate([own, l1[...], l2[...], l3[...]], 1)
    probs = weighed(pieces, held, scale, bias)
    weights = jnp.concatenate([(probs[:n] - label_of(marks, n)).astype(BF16), probs[n:].astype(BF16)], 0)
    out[...] = jnp.dot(pieces, weights, preferred_element_type=F32)


def far_kernel(scale, bias, dealt, far, h1, h2, h3, held, near, out):
    whole, n = h1.shape
    span = held.shape[1]
    rows = span // CORES
    features = whole // WIDTH
    w, level = lax.axis_index("width"), lax.axis_index("level")
    last = jnp.where((w < 2) == (level == 0), dealt[1 - level], far[...])
    pieces = jnp.concatenate([last, h1[...], h2[...], h3[...]], 1)
    probs = weighed(pieces, held, scale, bias)
    lane = lax.broadcasted_iota(jnp.int32, (n, span), 1)
    weights = jnp.concatenate(
        [
            jnp.where(lane // rows != w // 2, probs[:n], 0.0).astype(BF16),
            probs[n:].astype(BF16),
        ],
        0,
    )
    for to in range(WIDTH):
        at = slice(to * features, (to + 1) * features)
        total = near[at, :] + jnp.dot(pieces[at], weights, preferred_element_type=F32)
        total = total.astype(BF16)
        for core in range(CORES):
            out[core * WIDTH + to] = total[:, core * rows : (core + 1) * rows]


def per_device(images, texts, matches, scale, shift_bias):
    level = lax.axis_index("level")
    features, rows = images.shape[1], images.shape[0]
    span = CORES * rows
    quarter = span // WIDTH
    whole = WIDTH * features

    image, text = images.T, texts.T
    first = lax.axis_index("core") == 0
    to_deal, to_spread = jnp.where(first, image, text), jnp.where(first, text, image)
    noted = jnp.broadcast_to(matches.astype(BF16), (MARKS, rows))
    to_deal, to_spread = lax.optimization_barrier((to_deal, to_spread))
    dealt_other = swap_cores(to_spread)
    spread_other = swap_cores(jnp.concatenate([to_deal, noted], 0))
    params = pltpu.CompilerParams(vmem_limit_bytes=6 << 20)
    chunks = pl.pallas_call(
        deal_kernel,
        out_shape=jax.ShapeDtypeStruct((LEVELS * WIDTH, features, quarter), BF16),
        in_specs=[LOCAL] * 2,
        out_specs=LOCAL,
        compiler_params=params,
    )(to_deal, dealt_other)
    spread, marks = pl.pallas_call(
        spread_kernel,
        out_shape=[
            jax.ShapeDtypeStruct((WIDTH, features, span), BF16),
            jax.ShapeDtypeStruct((MARKS, span), F32),
        ],
        in_specs=[LOCAL] * 3,
        out_specs=[LOCAL] * 2,
        compiler_params=params,
    )(to_spread, matches, spread_other)
    dealt = lax.all_to_all(chunks, ("level", "width"), 0, 0).reshape(LEVELS, whole, quarter)
    own = lax.dynamic_index_in_dim(dealt, level, 0, False)
    pair = lax.dynamic_index_in_dim(dealt, 1 - level, 0, False)

    held = lax.all_to_all(spread, "width", 0, 0)
    held = held.reshape(whole, span)
    far = lax.ppermute(pair, ("row", "level"), far_route(lax.axis_size("row")))
    l1, l2, l3 = (along_line(own, d) for d in (1, 2, 3))

    piece = jax.ShapeDtypeStruct((whole, quarter), BF16)
    s1, s2, s3 = pl.pallas_call(
        halo_kernel,
        out_shape=[piece] * 3,
        in_specs=[LOCAL] * 2,
        out_specs=[LOCAL] * 3,
        compiler_params=params,
        cost_estimate=pl.CostEstimate(flops=10 * 10**9, bytes_accessed=2 << 20, transcendentals=0),
    )(pair, far)
    h1, h2, h3 = along_line(s3, 1), along_line(s2, 2), along_line(s1, 3)

    cost = pl.CostEstimate(
        flops=2 * whole * PIECES * quarter * span, bytes_accessed=5 << 20, transcendentals=0
    )
    params = pltpu.CompilerParams(vmem_limit_bytes=12 << 20)
    near = pl.pallas_call(
        near_kernel,
        out_shape=jax.ShapeDtypeStruct((whole, span), F32),
        in_specs=[SMEM, SMEM] + [LOCAL] * 6,
        out_specs=LOCAL,
        compiler_params=params,
        cost_estimate=cost,
    )(scale, shift_bias, marks, dealt, l1, l2, l3, held)
    partial = pl.pallas_call(
        far_kernel,
        out_shape=jax.ShapeDtypeStruct((CORES * WIDTH, features, rows), BF16),
        in_specs=[SMEM, SMEM] + [LOCAL] * 7,
        out_specs=LOCAL,
        compiler_params=params,
        cost_estimate=cost,
    )(scale, shift_bias, dealt, far, h1, h2, h3, held, near)
    terms = lax.all_to_all(partial, ("core", "width"), 0, 0).astype(F32)
    grad_text = terms[0] + terms[1] + terms[2] + terms[3]
    grad_image = terms[4] + terms[5] + terms[6] + terms[7]
    return (scale[0] * grad_image).T, (scale[0] * grad_text).T


def solution(mesh):
    deep = mesh.shape["tour"] // (LEVELS * LINE * CORES)
    fine = Mesh(
        mesh.devices.reshape(deep, LEVELS, LINE, CORES, WIDTH),
        ("row", "level", "x", "core", "width"),
    )
    rows, split = ("row", "level", "x", "core"), "width"
    return jax.shard_map(
        per_device,
        mesh=fine,
        in_specs=(P(rows, split), P(rows, split), P(rows, None), P(), P()),
        out_specs=(P(rows, split), P(rows, split)),
        check_vma=False,
    )
```

```python
import jax
import jax.numpy as jnp
from jax import lax
from jax.experimental import pallas as pl
from jax.experimental.pallas import tpu as pltpu
from jax.sharding import Mesh, PartitionSpec as P

CORES = 2
WIDTH = 4
LEVELS = 2
LINE = 4
BF16 = jnp.bfloat16
F32 = jnp.float32
SMEM = pl.BlockSpec(memory_space=pltpu.SMEM)
LOCAL = pl.BlockSpec(memory_space=pltpu.VMEM)
HBM = pl.BlockSpec(memory_space=pl.ANY)
PIECES = 2 * LINE
MARKS = 16


def swap_cores(block):
    return lax.ppermute(block, "core", [(0, 1), (1, 0)])


def along_line(block, turn):
    return lax.ppermute(block, "x", [(i ^ turn, i) for i in range(LINE)])


def far_route(rows):
    route = []
    for i in range(rows):
        route += [(2 * i, 2 * ((i + 1) % rows)), (2 * i + 1, 2 * ((i - 1) % rows) + 1)]
    return route


def deal_kernel(image, text, chunks, held, sems):
    features, rows = image.shape
    n, half = rows // WIDTH, features // 2
    copies = [
        pltpu.make_async_copy(source, held.at[i], sems.at[i])
        for i, source in enumerate((image, text))
    ]
    for copy in copies:
        copy.start()
    for core in range(CORES):
        copies[core].wait()
        for w in range(WIDTH):
            part = held[core, :, w * n : (w + 1) * n]
            part = jnp.concatenate([part[:half], part[half:]], 1)
            for level in range(LEVELS):
                chunks[(level * CORES + core) * WIDTH + w] = part


def gather_kernel(dealt, own, pair):
    half, n = dealt.shape[1], dealt.shape[2] // 2
    level = lax.axis_index("level")
    for out, at in ((own, level), (pair, 1 - level)):
        for w in range(WIDTH):
            left = dealt[at * CORES * WIDTH + w]
            right = dealt[(at * CORES + 1) * WIDTH + w]
            out[2 * w * half : (2 * w + 1) * half] = jnp.concatenate([left[:, :n], right[:, :n]], 1)
            out[(2 * w + 1) * half : (2 * w + 2) * half] = jnp.concatenate(
                [left[:, n:], right[:, n:]], 1
            )


def spread_kernel(mine, matches, other, spread, marks):
    features, rows = mine.shape
    first = lax.axis_index("core") == 0
    own, others = mine[...], other[:features, :]
    full = (jnp.where(first, own, others), jnp.where(first, others, own))
    for i in range(WIDTH):
        spread[i, :, :rows] = full[0]
        spread[i, :, rows:] = full[1]
    own_marks = jnp.broadcast_to(matches[...].astype(F32), (MARKS, rows))
    other_marks = other[features:, :].astype(F32)
    marks[:, :rows] = jnp.where(first, own_marks, other_marks)
    marks[:, rows:] = jnp.where(first, other_marks, own_marks)


def weighed(pieces, held, scale, bias):
    logits = lax.dot_general(
        pieces, held[...], (((0,), (0,)), ((), ())), preferred_element_type=F32
    )
    return jax.nn.sigmoid(scale[0] * logits + bias[0])


def halo_kernel(pair, far, *outs):
    x, level = lax.axis_index("x"), lax.axis_index("level")
    for turn, out in enumerate(outs, 1):
        higher = (x ^ turn) > x
        out[...] = jnp.where(higher == (level == 0), pair[...], far[...])


def label_of(marks, n):
    span = marks.shape[1]
    rows = span // CORES
    first, w = lax.axis_index("core") == 0, lax.axis_index("width")
    down = lax.broadcasted_iota(jnp.int32, (n, 1), 0)
    lane = lax.broadcasted_iota(jnp.int32, (1, span), 1)
    part = n // CORES
    block, row = down // part, w * part + down % part
    mark = jnp.where(lane == block * rows + row, marks[0:1, :], 0.0)
    have = jnp.where(first, jnp.sum(mark, axis=1, keepdims=True), row.astype(F32))
    goal = jnp.where(first, (lane % rows).astype(F32), marks[0:1, :])
    return ((have == goal) & (lane // rows == block)).astype(F32)


def weighed(pieces, held, scale, bias):
    logits = lax.dot_general(
        pieces, held[...], (((0,), (0,)), ((), ())), preferred_element_type=F32
    )
    return jax.nn.sigmoid(scale[0] * logits + bias[0])


def halo_kernel(pair, far, *outs):
    x, level = lax.axis_index("x"), lax.axis_index("level")
    for turn, out in enumerate(outs, 1):
        higher = (x ^ turn) > x
        out[...] = jnp.where(higher == (level == 0), pair[...], far[...])


def near_kernel(scale, bias, marks, own, l2, l3, l1, held, out):
    n = l1.shape[1]
    pieces = jnp.concatenate([own[...], l1[...], l2[...], l3[...]], 1)
    probs = weighed(pieces, held, scale, bias)
    weights = jnp.concatenate([(probs[:n] - label_of(marks, n)).astype(BF16), probs[n:].astype(BF16)], 0)
    out[...] = jnp.dot(pieces, weights, preferred_element_type=F32)


def far_kernel(scale, bias, pair, far, h2, h1, h3, held, near, out):
    whole, n = h1.shape
    span = held.shape[1]
    rows = span // CORES
    features = whole // WIDTH
    level = lax.axis_index("level")
    side = lax.broadcasted_iota(jnp.int32, (whole, n), 1) < n // CORES
    last = jnp.where(side == (level == 0), pair[...], far[...])
    pieces = jnp.concatenate([last, h1[...], h2[...], h3[...]], 1)
    probs = weighed(pieces, held, scale, bias)
    lane = lax.broadcasted_iota(jnp.int32, (n, span), 1)
    down = lax.broadcasted_iota(jnp.int32, (n, span), 0)
    met = lane // rows != down // (n // CORES)
    weights = jnp.concatenate(
        [
            jnp.where(met, probs[:n], 0.0).astype(BF16),
            probs[n:].astype(BF16),
        ],
        0,
    )
    for to in range(WIDTH):
        at = slice(to * features, (to + 1) * features)
        total = near[at, :] + jnp.dot(pieces[at], weights, preferred_element_type=F32)
        total = total.astype(BF16)
        for core in range(CORES):
            out[core * WIDTH + to] = total[:, core * rows : (core + 1) * rows]


def per_device(images, texts, matches, scale, shift_bias):
    features, rows = images.shape[1], images.shape[0]
    span = CORES * rows
    quarter = span // WIDTH
    whole = WIDTH * features

    image, text = images.T, texts.T
    piece = jax.ShapeDtypeStruct((whole, quarter), BF16)
    chunks = pl.pallas_call(
        deal_kernel,
        out_shape=jax.ShapeDtypeStruct((LEVELS * CORES * WIDTH, features // 2, quarter), BF16),
        in_specs=[HBM] * 2,
        out_specs=LOCAL,
        scratch_shapes=[
            pltpu.VMEM((CORES, features, rows), BF16),
            pltpu.SemaphoreType.DMA((CORES,)),
        ],
        compiler_params=pltpu.CompilerParams(vmem_limit_bytes=60 << 20),
    )(image, text)
    dealt = lax.all_to_all(chunks, ("level", "core", "width"), 0, 0)

    params = pltpu.CompilerParams(vmem_limit_bytes=6 << 20)
    first = lax.axis_index("core") == 0
    noted = jnp.broadcast_to(matches.astype(BF16), (MARKS, rows))
    other = swap_cores(jnp.concatenate([jnp.where(first, image, text), noted], 0))
    spread, marks = pl.pallas_call(
        spread_kernel,
        out_shape=[
            jax.ShapeDtypeStruct((WIDTH, features, span), BF16),
            jax.ShapeDtypeStruct((MARKS, span), F32),
        ],
        in_specs=[LOCAL] * 3,
        out_specs=[LOCAL] * 2,
        compiler_params=params,
    )(jnp.where(first, text, image), matches, other)
    own, pair = pl.pallas_call(
        gather_kernel,
        out_shape=[piece] * 2,
        in_specs=[LOCAL],
        out_specs=[LOCAL] * 2,
        compiler_params=params,
    )(dealt)

    held = lax.all_to_all(spread, "width", 0, 0)
    held = held.reshape(whole, span)
    far = lax.ppermute(pair, ("row", "level"), far_route(lax.axis_size("row")))
    l1, l2, l3 = (along_line(own, d) for d in (1, 2, 3))

    s1, s2, s3 = pl.pallas_call(
        halo_kernel,
        out_shape=[piece] * 3,
        in_specs=[LOCAL] * 2,
        out_specs=[LOCAL] * 3,
        compiler_params=params,
        cost_estimate=pl.CostEstimate(flops=10 * 10**9, bytes_accessed=2 << 20, transcendentals=0),
    )(pair, far)
    h1, h2, h3 = along_line(s1, 1), along_line(s2, 2), along_line(s3, 3)

    cost = pl.CostEstimate(
        flops=2 * whole * PIECES * quarter * span, bytes_accessed=5 << 20, transcendentals=0
    )
    params = pltpu.CompilerParams(vmem_limit_bytes=12 << 20)
    near = pl.pallas_call(
        near_kernel,
        out_shape=jax.ShapeDtypeStruct((whole, span), F32),
        in_specs=[SMEM, SMEM] + [LOCAL] * 6,
        out_specs=LOCAL,
        compiler_params=params,
        cost_estimate=cost,
    )(scale, shift_bias, marks, own, l2, l3, l1, held)
    partial = pl.pallas_call(
        far_kernel,
        out_shape=jax.ShapeDtypeStruct((CORES * WIDTH, features, rows), BF16),
        in_specs=[SMEM, SMEM] + [LOCAL] * 7,
        out_specs=LOCAL,
        compiler_params=params,
        cost_estimate=cost,
    )(scale, shift_bias, pair, far, h2, h1, h3, held, near)
    terms = lax.all_to_all(partial, ("core", "width"), 0, 0).astype(F32)
    grad_text = terms[0] + terms[1] + terms[2] + terms[3]
    grad_image = terms[4] + terms[5] + terms[6] + terms[7]
    return (scale[0] * grad_image).T, (scale[0] * grad_text).T


def solution(mesh):
    deep = mesh.shape["tour"] // (LEVELS * LINE * CORES)
    fine = Mesh(
        mesh.devices.reshape(deep, LEVELS, LINE, CORES, WIDTH),
        ("row", "level", "x", "core", "width"),
    )
    rows, split = ("row", "level", "x", "core"), "width"
    return jax.shard_map(
        per_device,
        mesh=fine,
        in_specs=(P(rows, split), P(rows, split), P(rows, None), P(), P()),
        out_specs=(P(rows, split), P(rows, split)),
        check_vma=False,
    )
```

```python
import jax
import jax.numpy as jnp
from jax import lax
from jax.experimental import pallas as pl
from jax.experimental.pallas import tpu as pltpu
from jax.sharding import Mesh, PartitionSpec as P

CORES = 2
WIDTH = 4
LEVELS = 2
LINE = 4
BF16 = jnp.bfloat16
F32 = jnp.float32
SMEM = pl.BlockSpec(memory_space=pltpu.SMEM)
LOCAL = pl.BlockSpec(memory_space=pltpu.VMEM)
HBM = pl.BlockSpec(memory_space=pl.ANY)
PIECES = 2 * LINE
MARKS = 16


def swap_cores(block):
    return lax.ppermute(block, "core", [(0, 1), (1, 0)])


def along_line(block, turn):
    return lax.ppermute(block, "x", [(i ^ turn, i) for i in range(LINE)])


def far_route(rows):
    route = []
    for i in range(rows):
        route += [(2 * i, 2 * ((i + 1) % rows)), (2 * i + 1, 2 * ((i - 1) % rows) + 1)]
    return route


def deal_kernel(image, text, chunks, held, sems):
    features, rows = image.shape
    n, half = rows // WIDTH, features // 2
    copies = [
        pltpu.make_async_copy(source, held.at[i], sems.at[i])
        for i, source in enumerate((image, text))
    ]
    for copy in copies:
        copy.start()
    for core in range(CORES):
        copies[core].wait()
        for w in range(WIDTH):
            part = held[core, :, w * n : (w + 1) * n]
            part = jnp.concatenate([part[:half], part[half:]], 1)
            for level in range(LEVELS):
                chunks[(level * CORES + core) * WIDTH + w] = part


def gather_kernel(dealt, own, pair):
    half, n = dealt.shape[1], dealt.shape[2] // 2
    level = lax.axis_index("level")
    for out, at in ((own, level), (pair, 1 - level)):
        for w in range(WIDTH):
            left = dealt[at * CORES * WIDTH + w]
            right = dealt[(at * CORES + 1) * WIDTH + w]
            out[2 * w * half : (2 * w + 1) * half] = jnp.concatenate([left[:, :n], right[:, :n]], 1)
            out[(2 * w + 1) * half : (2 * w + 2) * half] = jnp.concatenate(
                [left[:, n:], right[:, n:]], 1
            )


def spread_kernel(mine, matches, other, spread, marks):
    features, rows = mine.shape
    first = lax.axis_index("core") == 0
    own, others = mine[...], other[:features, :]
    full = (jnp.where(first, own, others), jnp.where(first, others, own))
    for i in range(WIDTH):
        spread[i, :, :rows] = full[0]
        spread[i, :, rows:] = full[1]
    own_marks = jnp.broadcast_to(matches[...].astype(F32), (MARKS, rows))
    other_marks = other[features:, :].astype(F32)
    marks[:, :rows] = jnp.where(first, own_marks, other_marks)
    marks[:, rows:] = jnp.where(first, other_marks, own_marks)


def weighed(pieces, held, scale, bias):
    logits = lax.dot_general(
        pieces, held[...], (((0,), (0,)), ((), ())), preferred_element_type=F32
    )
    return jax.nn.sigmoid(scale[0] * logits + bias[0])


def halo_kernel(pair, far, *outs):
    x, level = lax.axis_index("x"), lax.axis_index("level")
    for turn, out in enumerate(outs, 1):
        higher = (x ^ turn) > x
        out[...] = jnp.where(higher == (level == 0), pair[...], far[...])


def label_of(marks, n):
    span = marks.shape[1]
    rows = span // CORES
    first, w = lax.axis_index("core") == 0, lax.axis_index("width")
    down = lax.broadcasted_iota(jnp.int32, (n, 1), 0)
    lane = lax.broadcasted_iota(jnp.int32, (1, span), 1)
    part = n // CORES
    block, row = down // part, w * part + down % part
    mark = jnp.where(lane == block * rows + row, marks[0:1, :], 0.0)
    have = jnp.where(first, jnp.sum(mark, axis=1, keepdims=True), row.astype(F32))
    goal = jnp.where(first, (lane % rows).astype(F32), marks[0:1, :])
    return ((have == goal) & (lane // rows == block)).astype(F32)


def near_kernel(scale, bias, marks, own, l2, l3, l1, held, out):
    n = l1.shape[1]
    pieces = jnp.concatenate([own[...], l1[...], l2[...], l3[...]], 1)
    probs = weighed(pieces, held, scale, bias)
    weights = jnp.concatenate([(probs[:n] - label_of(marks, n)).astype(BF16), probs[n:].astype(BF16)], 0)
    out[...] = jnp.dot(pieces, weights, preferred_element_type=F32)


def far_kernel(scale, bias, pair, far, h2, h1, h3, held, near, out):
    whole, n = h1.shape
    span = held.shape[1]
    rows = span // CORES
    features = whole // WIDTH
    level = lax.axis_index("level")
    side = lax.broadcasted_iota(jnp.int32, (whole, n), 1) < n // CORES
    last = jnp.where(side == (level == 0), pair[...], far[...])
    pieces = jnp.concatenate([last, h1[...], h2[...], h3[...]], 1)
    probs = weighed(pieces, held, scale, bias)
    lane = lax.broadcasted_iota(jnp.int32, (n, span), 1)
    down = lax.broadcasted_iota(jnp.int32, (n, span), 0)
    met = lane // rows != down // (n // CORES)
    weights = jnp.concatenate(
        [
            jnp.where(met, probs[:n], 0.0).astype(BF16),
            probs[n:].astype(BF16),
        ],
        0,
    )
    for to in range(WIDTH):
        at = slice(to * features, (to + 1) * features)
        total = near[at, :] + jnp.dot(pieces[at], weights, preferred_element_type=F32)
        total = total.astype(BF16)
        for core in range(CORES):
            out[core * WIDTH + to] = total[:, core * rows : (core + 1) * rows]


def per_device(images, texts, matches, scale, shift_bias):
    features, rows = images.shape[1], images.shape[0]
    span = CORES * rows
    quarter = span // WIDTH
    whole = WIDTH * features

    image, text = images.T, texts.T
    piece = jax.ShapeDtypeStruct((whole, quarter), BF16)
    chunks = pl.pallas_call(
        deal_kernel,
        out_shape=jax.ShapeDtypeStruct((LEVELS * CORES * WIDTH, features // 2, quarter), BF16),
        in_specs=[HBM] * 2,
        out_specs=LOCAL,
        scratch_shapes=[
            pltpu.VMEM((CORES, features, rows), BF16),
            pltpu.SemaphoreType.DMA((CORES,)),
        ],
        compiler_params=pltpu.CompilerParams(vmem_limit_bytes=60 << 20),
    )(image, text)
    dealt = lax.all_to_all(chunks, ("level", "core", "width"), 0, 0)

    params = pltpu.CompilerParams(vmem_limit_bytes=6 << 20)
    first = lax.axis_index("core") == 0
    noted = jnp.broadcast_to(matches.astype(BF16), (MARKS, rows))
    other = swap_cores(jnp.concatenate([jnp.where(first, image, text), noted], 0))
    spread, marks = pl.pallas_call(
        spread_kernel,
        out_shape=[
            jax.ShapeDtypeStruct((WIDTH, features, span), BF16),
            jax.ShapeDtypeStruct((MARKS, span), F32),
        ],
        in_specs=[LOCAL] * 3,
        out_specs=[LOCAL] * 2,
        compiler_params=params,
    )(jnp.where(first, text, image), matches, other)
    dealt, spread = lax.optimization_barrier((dealt, spread))
    own, pair = pl.pallas_call(
        gather_kernel,
        out_shape=[piece] * 2,
        in_specs=[LOCAL],
        out_specs=[LOCAL] * 2,
        compiler_params=params,
    )(dealt)

    held = lax.all_to_all(spread, "width", 0, 0)
    held = held.reshape(whole, span)
    far = lax.ppermute(pair, ("row", "level"), far_route(lax.axis_size("row")))
    l1, l2, l3 = (along_line(own, d) for d in (1, 2, 3))

    s1, s2, s3 = pl.pallas_call(
        halo_kernel,
        out_shape=[piece] * 3,
        in_specs=[LOCAL] * 2,
        out_specs=[LOCAL] * 3,
        compiler_params=params,
        cost_estimate=pl.CostEstimate(flops=15 * 10**9, bytes_accessed=2 << 20, transcendentals=0),
    )(pair, far)
    h1, h2, h3 = along_line(s1, 1), along_line(s2, 2), along_line(s3, 3)

    cost = pl.CostEstimate(
        flops=2 * whole * PIECES * quarter * span, bytes_accessed=5 << 20, transcendentals=0
    )
    params = pltpu.CompilerParams(vmem_limit_bytes=12 << 20)
    near = pl.pallas_call(
        near_kernel,
        out_shape=jax.ShapeDtypeStruct((whole, span), F32),
        in_specs=[SMEM, SMEM] + [LOCAL] * 6,
        out_specs=LOCAL,
        compiler_params=params,
        cost_estimate=cost,
    )(scale, shift_bias, marks, own, l2, l3, l1, held)
    partial = pl.pallas_call(
        far_kernel,
        out_shape=jax.ShapeDtypeStruct((CORES * WIDTH, features, rows), BF16),
        in_specs=[SMEM, SMEM] + [LOCAL] * 7,
        out_specs=LOCAL,
        compiler_params=params,
        cost_estimate=cost,
    )(scale, shift_bias, pair, far, h2, h1, h3, held, near)
    terms = lax.all_to_all(partial, ("core", "width"), 0, 0).astype(F32)
    grad_text = terms[0] + terms[1] + terms[2] + terms[3]
    grad_image = terms[4] + terms[5] + terms[6] + terms[7]
    return (scale[0] * grad_image).T, (scale[0] * grad_text).T


def solution(mesh):
    deep = mesh.shape["tour"] // (LEVELS * LINE * CORES)
    fine = Mesh(
        mesh.devices.reshape(deep, LEVELS, LINE, CORES, WIDTH),
        ("row", "level", "x", "core", "width"),
    )
    rows, split = ("row", "level", "x", "core"), "width"
    return jax.shard_map(
        per_device,
        mesh=fine,
        in_specs=(P(rows, split), P(rows, split), P(rows, None), P(), P()),
        out_specs=(P(rows, split), P(rows, split)),
        check_vma=False,
    )
```

```python
import jax
import jax.numpy as jnp
from jax import lax
from jax.experimental import pallas as pl
from jax.experimental.pallas import tpu as pltpu
from jax.sharding import Mesh, PartitionSpec as P

CORES = 2
WIDTH = 4
LEVELS = 2
LINE = 4
BF16 = jnp.bfloat16
F32 = jnp.float32
SMEM = pl.BlockSpec(memory_space=pltpu.SMEM)
LOCAL = pl.BlockSpec(memory_space=pltpu.VMEM)
HBM = pl.BlockSpec(memory_space=pl.ANY)
PIECES = 2 * LINE
MARKS = 16


def swap_cores(block):
    return lax.ppermute(block, "core", [(0, 1), (1, 0)])


def along_line(block, turn):
    return lax.ppermute(block, "x", [((i + turn) % LINE, i) for i in range(LINE)])


def far_route(rows):
    route = []
    for i in range(rows):
        route += [(2 * i, 2 * ((i + 1) % rows)), (2 * i + 1, 2 * ((i - 1) % rows) + 1)]
    return route


def deal_kernel(image, text, chunks, held, sems):
    features, rows = image.shape
    n, half = rows // WIDTH, features // 2
    copies = [
        pltpu.make_async_copy(source, held.at[i], sems.at[i])
        for i, source in enumerate((image, text))
    ]
    for copy in copies:
        copy.start()
    for core in range(CORES):
        copies[core].wait()
        for w in range(WIDTH):
            part = held[core, :, w * n : (w + 1) * n]
            part = jnp.concatenate([part[:half], part[half:]], 1)
            for level in range(LEVELS):
                chunks[(level * CORES + core) * WIDTH + w] = part


def gather_kernel(dealt, own, pair):
    half, n = dealt.shape[1], dealt.shape[2] // 2
    level = lax.axis_index("level")
    for out, at in ((own, level), (pair, 1 - level)):
        for w in range(WIDTH):
            left = dealt[at * CORES * WIDTH + w]
            right = dealt[(at * CORES + 1) * WIDTH + w]
            out[2 * w * half : (2 * w + 1) * half] = jnp.concatenate([left[:, :n], right[:, :n]], 1)
            out[(2 * w + 1) * half : (2 * w + 2) * half] = jnp.concatenate(
                [left[:, n:], right[:, n:]], 1
            )


def spread_kernel(mine, matches, other, spread, marks):
    features, rows = mine.shape
    first = lax.axis_index("core") == 0
    own, others = mine[...], other[:features, :]
    full = (jnp.where(first, own, others), jnp.where(first, others, own))
    for i in range(WIDTH):
        spread[i, :, :rows] = full[0]
        spread[i, :, rows:] = full[1]
    own_marks = jnp.broadcast_to(matches[...].astype(F32), (MARKS, rows))
    other_marks = other[features:, :].astype(F32)
    marks[:, :rows] = jnp.where(first, own_marks, other_marks)
    marks[:, rows:] = jnp.where(first, other_marks, own_marks)


def weighed(pieces, held, scale, bias):
    logits = lax.dot_general(
        pieces, held[...], (((0,), (0,)), ((), ())), preferred_element_type=F32
    )
    return jax.nn.sigmoid(scale[0] * logits + bias[0])


def halo_kernel(pair, far, *outs):
    x, level = lax.axis_index("x"), lax.axis_index("level")
    for turn, out in enumerate(outs, 1):
        higher = lax.rem(x + LINE - turn, LINE) > x
        out[...] = jnp.where(higher == (level == 0), pair[...], far[...])


def label_of(marks, n):
    span = marks.shape[1]
    rows = span // CORES
    first, w = lax.axis_index("core") == 0, lax.axis_index("width")
    down = lax.broadcasted_iota(jnp.int32, (n, 1), 0)
    lane = lax.broadcasted_iota(jnp.int32, (1, span), 1)
    part = n // CORES
    block, row = down // part, w * part + down % part
    mark = jnp.where(lane == block * rows + row, marks[0:1, :], 0.0)
    have = jnp.where(first, jnp.sum(mark, axis=1, keepdims=True), row.astype(F32))
    goal = jnp.where(first, (lane % rows).astype(F32), marks[0:1, :])
    return ((have == goal) & (lane // rows == block)).astype(F32)


def near_kernel(scale, bias, marks, own, l2, l3, l1, held, out):
    n = l1.shape[1]
    pieces = jnp.concatenate([own[...], l1[...], l2[...], l3[...]], 1)
    probs = weighed(pieces, held, scale, bias)
    weights = jnp.concatenate([(probs[:n] - label_of(marks, n)).astype(BF16), probs[n:].astype(BF16)], 0)
    out[...] = jnp.dot(pieces, weights, preferred_element_type=F32)


def far_kernel(scale, bias, pair, far, h2, h1, h3, held, near, out):
    whole, n = h1.shape
    span = held.shape[1]
    rows = span // CORES
    features = whole // WIDTH
    level = lax.axis_index("level")
    side = lax.broadcasted_iota(jnp.int32, (whole, n), 1) < n // CORES
    last = jnp.where(side == (level == 0), pair[...], far[...])
    pieces = jnp.concatenate([last, h1[...], h2[...], h3[...]], 1)
    probs = weighed(pieces, held, scale, bias)
    lane = lax.broadcasted_iota(jnp.int32, (n, span), 1)
    down = lax.broadcasted_iota(jnp.int32, (n, span), 0)
    met = lane // rows != down // (n // CORES)
    weights = jnp.concatenate(
        [
            jnp.where(met, probs[:n], 0.0).astype(BF16),
            probs[n:].astype(BF16),
        ],
        0,
    )
    for to in range(WIDTH):
        at = slice(to * features, (to + 1) * features)
        total = near[at, :] + jnp.dot(pieces[at], weights, preferred_element_type=F32)
        total = total.astype(BF16)
        for core in range(CORES):
            out[core * WIDTH + to] = total[:, core * rows : (core + 1) * rows]


def per_device(images, texts, matches, scale, shift_bias):
    features, rows = images.shape[1], images.shape[0]
    span = CORES * rows
    quarter = span // WIDTH
    whole = WIDTH * features

    image, text = images.T, texts.T
    piece = jax.ShapeDtypeStruct((whole, quarter), BF16)
    chunks = pl.pallas_call(
        deal_kernel,
        out_shape=jax.ShapeDtypeStruct((LEVELS * CORES * WIDTH, features // 2, quarter), BF16),
        in_specs=[HBM] * 2,
        out_specs=LOCAL,
        scratch_shapes=[
            pltpu.VMEM((CORES, features, rows), BF16),
            pltpu.SemaphoreType.DMA((CORES,)),
        ],
        compiler_params=pltpu.CompilerParams(vmem_limit_bytes=60 << 20),
    )(image, text)
    dealt = lax.all_to_all(chunks, ("level", "core", "width"), 0, 0)

    params = pltpu.CompilerParams(vmem_limit_bytes=6 << 20)
    first = lax.axis_index("core") == 0
    noted = jnp.broadcast_to(matches.astype(BF16), (MARKS, rows))
    other = swap_cores(jnp.concatenate([jnp.where(first, image, text), noted], 0))
    spread, marks = pl.pallas_call(
        spread_kernel,
        out_shape=[
            jax.ShapeDtypeStruct((WIDTH, features, span), BF16),
            jax.ShapeDtypeStruct((MARKS, span), F32),
        ],
        in_specs=[LOCAL] * 3,
        out_specs=[LOCAL] * 2,
        compiler_params=params,
    )(jnp.where(first, text, image), matches, other)
    dealt, spread = lax.optimization_barrier((dealt, spread))
    own, pair = pl.pallas_call(
        gather_kernel,
        out_shape=[piece] * 2,
        in_specs=[LOCAL],
        out_specs=[LOCAL] * 2,
        compiler_params=params,
    )(dealt)

    held = lax.all_to_all(spread, "width", 0, 0)
    held = held.reshape(whole, span)
    far = lax.ppermute(pair, ("row", "level"), far_route(lax.axis_size("row")))
    l1, l2, l3 = (along_line(own, d) for d in (1, 2, 3))

    s1, s2, s3 = pl.pallas_call(
        halo_kernel,
        out_shape=[piece] * 3,
        in_specs=[LOCAL] * 2,
        out_specs=[LOCAL] * 3,
        compiler_params=params,
        cost_estimate=pl.CostEstimate(flops=15 * 10**9, bytes_accessed=2 << 20, transcendentals=0),
    )(pair, far)
    h1, h2, h3 = along_line(s1, 1), along_line(s2, 2), along_line(s3, 3)

    cost = pl.CostEstimate(
        flops=2 * whole * PIECES * quarter * span, bytes_accessed=5 << 20, transcendentals=0
    )
    params = pltpu.CompilerParams(vmem_limit_bytes=12 << 20)
    near = pl.pallas_call(
        near_kernel,
        out_shape=jax.ShapeDtypeStruct((whole, span), F32),
        in_specs=[SMEM, SMEM] + [LOCAL] * 6,
        out_specs=LOCAL,
        compiler_params=params,
        cost_estimate=cost,
    )(scale, shift_bias, marks, own, l2, l3, l1, held)
    partial = pl.pallas_call(
        far_kernel,
        out_shape=jax.ShapeDtypeStruct((CORES * WIDTH, features, rows), BF16),
        in_specs=[SMEM, SMEM] + [LOCAL] * 7,
        out_specs=LOCAL,
        compiler_params=params,
        cost_estimate=cost,
    )(scale, shift_bias, pair, far, h2, h1, h3, held, near)
    terms = lax.all_to_all(partial, ("core", "width"), 0, 0).astype(F32)
    grad_text = terms[0] + terms[1] + terms[2] + terms[3]
    grad_image = terms[4] + terms[5] + terms[6] + terms[7]
    return (scale[0] * grad_image).T, (scale[0] * grad_text).T


def solution(mesh):
    deep = mesh.shape["tour"] // (LEVELS * LINE * CORES)
    fine = Mesh(
        mesh.devices.reshape(deep, LEVELS, LINE, CORES, WIDTH),
        ("row", "level", "x", "core", "width"),
    )
    rows, split = ("row", "level", "x", "core"), "width"
    return jax.shard_map(
        per_device,
        mesh=fine,
        in_specs=(P(rows, split), P(rows, split), P(rows, None), P(), P()),
        out_specs=(P(rows, split), P(rows, split)),
        check_vma=False,
    )
```

```python
import jax
import jax.numpy as jnp
from jax import lax
from jax.experimental import pallas as pl
from jax.experimental.pallas import tpu as pltpu
from jax.sharding import Mesh, PartitionSpec as P

CORES = 2
WIDTH = 4
LEVELS = 2
LINE = 4
BF16 = jnp.bfloat16
F32 = jnp.float32
SMEM = pl.BlockSpec(memory_space=pltpu.SMEM)
LOCAL = pl.BlockSpec(memory_space=pltpu.VMEM)
HBM = pl.BlockSpec(memory_space=pl.ANY)
PIECES = 2 * LINE
MARKS = 16


def swap_cores(block):
    return lax.ppermute(block, "core", [(0, 1), (1, 0)])


def along_line(block, turn):
    return lax.ppermute(block, "x", [((i + turn) % LINE, i) for i in range(LINE)])


def far_route(rows):
    route = []
    for i in range(rows):
        route += [(2 * i, 2 * ((i + 1) % rows)), (2 * i + 1, 2 * ((i - 1) % rows) + 1)]
    return route


def deal_kernel(image, text, chunks, held, staged, sems, out_sems):
    features, rows = image.shape
    n, half = rows // WIDTH, features // 2
    copies = [
        pltpu.make_async_copy(source, held.at[i], sems.at[i])
        for i, source in enumerate((image, text))
    ]
    for copy in copies:
        copy.start()
    sent = []
    for core in range(CORES):
        copies[core].wait()
        for w in range(WIDTH):
            part = held[core, :, w * n : (w + 1) * n]
            staged[core, w] = jnp.concatenate([part[:half], part[half:]], 1)
        for level in range(LEVELS):
            to = chunks.at[pl.ds((level * CORES + core) * WIDTH, WIDTH)]
            sent.append(
                pltpu.make_async_copy(staged.at[core], to, out_sems.at[level * CORES + core])
            )
            sent[-1].start()
    for copy in sent:
        copy.wait()


def gather_kernel(dealt, own, pair):
    half, n = dealt.shape[1], dealt.shape[2] // 2
    level = lax.axis_index("level")
    for out, at in ((own, level), (pair, 1 - level)):
        for w in range(WIDTH):
            left = dealt[at * CORES * WIDTH + w]
            right = dealt[(at * CORES + 1) * WIDTH + w]
            out[2 * w * half : (2 * w + 1) * half] = jnp.concatenate([left[:, :n], right[:, :n]], 1)
            out[(2 * w + 1) * half : (2 * w + 2) * half] = jnp.concatenate(
                [left[:, n:], right[:, n:]], 1
            )


def spread_kernel(mine, matches, other, spread, marks):
    features, rows = mine.shape
    first = lax.axis_index("core") == 0
    own, others = mine[...], other[:features, :]
    full = (jnp.where(first, own, others), jnp.where(first, others, own))
    for i in range(WIDTH):
        spread[i, :, :rows] = full[0]
        spread[i, :, rows:] = full[1]
    own_marks = jnp.broadcast_to(matches[...].astype(F32), (MARKS, rows))
    other_marks = other[features:, :].astype(F32)
    marks[:, :rows] = jnp.where(first, own_marks, other_marks)
    marks[:, rows:] = jnp.where(first, other_marks, own_marks)


def weighed(pieces, held, scale, bias):
    logits = lax.dot_general(
        pieces, held[...], (((0,), (0,)), ((), ())), preferred_element_type=F32
    )
    return jax.nn.sigmoid(scale[0] * logits + bias[0])


def halo_kernel(pair, far, o1, o2, o3, sems):
    x, level = lax.axis_index("x"), lax.axis_index("level")
    copies = []
    for turn, out in ((1, o1), (2, o2), (3, o3)):
        of_pair = (lax.rem(x + LINE - turn, LINE) > x) == (level == 0)
        mine = pltpu.make_async_copy(pair, out, sems.at[turn - 1])
        other = pltpu.make_async_copy(far, out, sems.at[turn - 1])
        pl.when(of_pair)(mine.start)
        pl.when(jnp.logical_not(of_pair))(other.start)
        copies.append(mine)
    for copy in copies:
        copy.wait()


def label_of(marks, n):
    span = marks.shape[1]
    rows = span // CORES
    first, w = lax.axis_index("core") == 0, lax.axis_index("width")
    down = lax.broadcasted_iota(jnp.int32, (n, 1), 0)
    lane = lax.broadcasted_iota(jnp.int32, (1, span), 1)
    part = n // CORES
    block, row = down // part, w * part + down % part
    mark = jnp.where(lane == block * rows + row, marks[0:1, :], 0.0)
    have = jnp.where(first, jnp.sum(mark, axis=1, keepdims=True), row.astype(F32))
    goal = jnp.where(first, (lane % rows).astype(F32), marks[0:1, :])
    return ((have == goal) & (lane // rows == block)).astype(F32)


def near_kernel(scale, bias, marks, own, l2, l3, l1, held, out):
    n = l1.shape[1]
    pieces = jnp.concatenate([own[...], l1[...], l2[...], l3[...]], 1)
    probs = weighed(pieces, held, scale, bias)
    weights = jnp.concatenate([(probs[:n] - label_of(marks, n)).astype(BF16), probs[n:].astype(BF16)], 0)
    out[...] = jnp.dot(pieces, weights, preferred_element_type=F32)


def far_kernel(scale, bias, pair, far, h2, h1, h3, held, near, out):
    whole, n = h1.shape
    span = held.shape[1]
    rows = span // CORES
    features = whole // WIDTH
    level = lax.axis_index("level")
    side = lax.broadcasted_iota(jnp.int32, (whole, n), 1) < n // CORES
    last = jnp.where(side == (level == 0), pair[...], far[...])
    pieces = jnp.concatenate([last, h1[...], h2[...], h3[...]], 1)
    probs = weighed(pieces, held, scale, bias)
    lane = lax.broadcasted_iota(jnp.int32, (n, span), 1)
    down = lax.broadcasted_iota(jnp.int32, (n, span), 0)
    met = lane // rows != down // (n // CORES)
    weights = jnp.concatenate(
        [
            jnp.where(met, probs[:n], 0.0).astype(BF16),
            probs[n:].astype(BF16),
        ],
        0,
    )
    for to in range(WIDTH):
        at = slice(to * features, (to + 1) * features)
        total = near[at, :] + jnp.dot(pieces[at], weights, preferred_element_type=F32)
        total = total.astype(BF16)
        for core in range(CORES):
            out[core * WIDTH + to] = total[:, core * rows : (core + 1) * rows]


def per_device(images, texts, matches, scale, shift_bias):
    features, rows = images.shape[1], images.shape[0]
    span = CORES * rows
    quarter = span // WIDTH
    whole = WIDTH * features

    image, text = images.T, texts.T
    piece = jax.ShapeDtypeStruct((whole, quarter), BF16)
    chunks = pl.pallas_call(
        deal_kernel,
        out_shape=jax.ShapeDtypeStruct((LEVELS * CORES * WIDTH, features // 2, quarter), BF16),
        in_specs=[HBM] * 2,
        out_specs=HBM,
        scratch_shapes=[
            pltpu.VMEM((CORES, features, rows), BF16),
            pltpu.VMEM((CORES, WIDTH, features // 2, quarter), BF16),
            pltpu.SemaphoreType.DMA((CORES,)),
            pltpu.SemaphoreType.DMA((LEVELS * CORES,)),
        ],
        compiler_params=pltpu.CompilerParams(vmem_limit_bytes=60 << 20),
    )(image, text)
    dealt = lax.all_to_all(chunks, ("level", "core", "width"), 0, 0)

    params = pltpu.CompilerParams(vmem_limit_bytes=6 << 20)
    first = lax.axis_index("core") == 0
    noted = jnp.broadcast_to(matches.astype(BF16), (MARKS, rows))
    other = swap_cores(jnp.concatenate([jnp.where(first, image, text), noted], 0))
    spread, marks = pl.pallas_call(
        spread_kernel,
        out_shape=[
            jax.ShapeDtypeStruct((WIDTH, features, span), BF16),
            jax.ShapeDtypeStruct((MARKS, span), F32),
        ],
        in_specs=[LOCAL] * 3,
        out_specs=[LOCAL] * 2,
        compiler_params=params,
    )(jnp.where(first, text, image), matches, other)
    dealt, spread = lax.optimization_barrier((dealt, spread))
    own, pair = pl.pallas_call(
        gather_kernel,
        out_shape=[piece] * 2,
        in_specs=[LOCAL],
        out_specs=[LOCAL] * 2,
        compiler_params=params,
    )(dealt)

    held = lax.all_to_all(spread, "width", 0, 0)
    held = held.reshape(whole, span)
    far = lax.ppermute(pair, ("row", "level"), far_route(lax.axis_size("row")))
    l1, l2, l3 = (along_line(own, d) for d in (1, 2, 3))

    s1, s2, s3 = pl.pallas_call(
        halo_kernel,
        out_shape=[piece] * 3,
        in_specs=[HBM] * 2,
        out_specs=[HBM] * 3,
        scratch_shapes=[pltpu.SemaphoreType.DMA((LINE - 1,))],
        compiler_params=params,
        cost_estimate=pl.CostEstimate(flops=15 * 10**9, bytes_accessed=2 << 20, transcendentals=0),
    )(pair, far)
    h1, h2, h3 = along_line(s1, 1), along_line(s2, 2), along_line(s3, 3)

    cost = pl.CostEstimate(
        flops=2 * whole * PIECES * quarter * span, bytes_accessed=5 << 20, transcendentals=0
    )
    params = pltpu.CompilerParams(vmem_limit_bytes=12 << 20)
    near = pl.pallas_call(
        near_kernel,
        out_shape=jax.ShapeDtypeStruct((whole, span), F32),
        in_specs=[SMEM, SMEM] + [LOCAL] * 6,
        out_specs=LOCAL,
        compiler_params=params,
        cost_estimate=cost,
    )(scale, shift_bias, marks, own, l2, l3, l1, held)
    partial = pl.pallas_call(
        far_kernel,
        out_shape=jax.ShapeDtypeStruct((CORES * WIDTH, features, rows), BF16),
        in_specs=[SMEM, SMEM] + [LOCAL] * 7,
        out_specs=LOCAL,
        compiler_params=params,
        cost_estimate=cost,
    )(scale, shift_bias, pair, far, h2, h1, h3, held, near)
    terms = lax.all_to_all(partial, ("core", "width"), 0, 0).astype(F32)
    grad_text = terms[0] + terms[1] + terms[2] + terms[3]
    grad_image = terms[4] + terms[5] + terms[6] + terms[7]
    return (scale[0] * grad_image).T, (scale[0] * grad_text).T


def solution(mesh):
    deep = mesh.shape["tour"] // (LEVELS * LINE * CORES)
    fine = Mesh(
        mesh.devices.reshape(deep, LEVELS, LINE, CORES, WIDTH),
        ("row", "level", "x", "core", "width"),
    )
    rows, split = ("row", "level", "x", "core"), "width"
    return jax.shard_map(
        per_device,
        mesh=fine,
        in_specs=(P(rows, split), P(rows, split), P(rows, None), P(), P()),
        out_specs=(P(rows, split), P(rows, split)),
        check_vma=False,
    )
```

```python
import jax
import jax.numpy as jnp
from jax import lax
from jax.experimental import pallas as pl
from jax.experimental.pallas import tpu as pltpu
from jax.sharding import Mesh, PartitionSpec as P

CORES = 2
WIDTH = 4
LEVELS = 2
LINE = 4
BF16 = jnp.bfloat16
F32 = jnp.float32
SMEM = pl.BlockSpec(memory_space=pltpu.SMEM)
LOCAL = pl.BlockSpec(memory_space=pltpu.VMEM)
HBM = pl.BlockSpec(memory_space=pl.ANY)
PIECES = 2 * LINE
MARKS = 16


def swap_cores(block):
    return lax.ppermute(block, "core", [(0, 1), (1, 0)])


def along_line(block, turn):
    return lax.ppermute(block, "x", [((i + turn) % LINE, i) for i in range(LINE)])


def far_route(rows):
    route = []
    for i in range(rows):
        route += [(2 * i, 2 * ((i + 1) % rows)), (2 * i + 1, 2 * ((i - 1) % rows) + 1)]
    return route


def deal_kernel(image, text, chunks, held, sems):
    features, rows = image.shape
    n, half = rows // WIDTH, features // 2
    copies = [
        pltpu.make_async_copy(source, held.at[i], sems.at[i])
        for i, source in enumerate((image, text))
    ]
    for copy in copies:
        copy.start()
    for core in range(CORES):
        copies[core].wait()
        for w in range(WIDTH):
            part = held[core, :, w * n : (w + 1) * n]
            part = jnp.concatenate([part[:half], part[half:]], 1)
            for level in range(LEVELS):
                chunks[(level * CORES + core) * WIDTH + w] = part


def gather_kernel(dealt, own, pair):
    half, n = dealt.shape[1], dealt.shape[2] // 2
    level = lax.axis_index("level")
    for out, at in ((own, level), (pair, 1 - level)):
        for w in range(WIDTH):
            left = dealt[at * CORES * WIDTH + w]
            right = dealt[(at * CORES + 1) * WIDTH + w]
            out[2 * w * half : (2 * w + 1) * half] = jnp.concatenate([left[:, :n], right[:, :n]], 1)
            out[(2 * w + 1) * half : (2 * w + 2) * half] = jnp.concatenate(
                [left[:, n:], right[:, n:]], 1
            )


def spread_kernel(mine, matches, other, spread, marks):
    features, rows = mine.shape
    first = lax.axis_index("core") == 0
    own, others = mine[...], other[:features, :]
    full = (jnp.where(first, own, others), jnp.where(first, others, own))
    for i in range(WIDTH):
        spread[i, :, :rows] = full[0]
        spread[i, :, rows:] = full[1]
    own_marks = jnp.broadcast_to(matches[...].astype(F32), (MARKS, rows))
    other_marks = other[features:, :].astype(F32)
    marks[:, :rows] = jnp.where(first, own_marks, other_marks)
    marks[:, rows:] = jnp.where(first, other_marks, own_marks)


def weighed(pieces, held, scale, bias):
    logits = lax.dot_general(
        pieces, held[...], (((0,), (0,)), ((), ())), preferred_element_type=F32
    )
    return jax.nn.sigmoid(scale[0] * logits + bias[0])


def halo_kernel(pair, far, *outs):
    x, level = lax.axis_index("x"), lax.axis_index("level")
    for turn, out in enumerate(outs, 1):
        higher = lax.rem(x + LINE - turn, LINE) > x
        out[...] = jnp.where(higher == (level == 0), pair[...], far[...])


def label_of(marks, n):
    span = marks.shape[1]
    rows = span // CORES
    first, w = lax.axis_index("core") == 0, lax.axis_index("width")
    down = lax.broadcasted_iota(jnp.int32, (n, 1), 0)
    lane = lax.broadcasted_iota(jnp.int32, (1, span), 1)
    part = n // CORES
    block, row = down // part, w * part + down % part
    mark = jnp.where(lane == block * rows + row, marks[0:1, :], 0.0)
    have = jnp.where(first, jnp.sum(mark, axis=1, keepdims=True), row.astype(F32))
    goal = jnp.where(first, (lane % rows).astype(F32), marks[0:1, :])
    return ((have == goal) & (lane // rows == block)).astype(F32)


def near_kernel(scale, bias, marks, own, pair, far, l2, l3, l1, held, out):
    whole, n = l1.shape
    span = held.shape[1]
    rows = span // CORES
    side = lax.broadcasted_iota(jnp.int32, (whole, n), 1) < n // CORES
    last = jnp.where(side == (lax.axis_index("level") == 0), pair[...], far[...])
    pieces = jnp.concatenate([own[...], l1[...], l2[...], l3[...], last], 1)
    probs = weighed(pieces, held, scale, bias)
    lane = lax.broadcasted_iota(jnp.int32, (n, span), 1)
    down = lax.broadcasted_iota(jnp.int32, (n, span), 0)
    met = lane // rows != down // (n // CORES)
    end = probs.shape[0] - n
    weights = jnp.concatenate(
        [
            (probs[:n] - label_of(marks, n)).astype(BF16),
            probs[n:end].astype(BF16),
            jnp.where(met, probs[end:], 0.0).astype(BF16),
        ],
        0,
    )
    out[...] = jnp.dot(pieces, weights, preferred_element_type=F32)


def far_kernel(scale, bias, h2, h1, h3, held, near, out):
    rows = held.shape[1] // CORES
    features = h1.shape[0] // WIDTH
    pieces = jnp.concatenate([h1[...], h2[...], h3[...]], 1)
    weights = weighed(pieces, held, scale, bias).astype(BF16)
    for to in range(WIDTH):
        at = slice(to * features, (to + 1) * features)
        total = near[at, :] + jnp.dot(pieces[at], weights, preferred_element_type=F32)
        total = total.astype(BF16)
        for core in range(CORES):
            out[core * WIDTH + to] = total[:, core * rows : (core + 1) * rows]


def per_device(images, texts, matches, scale, shift_bias):
    features, rows = images.shape[1], images.shape[0]
    span = CORES * rows
    quarter = span // WIDTH
    whole = WIDTH * features

    image, text = images.T, texts.T
    piece = jax.ShapeDtypeStruct((whole, quarter), BF16)
    chunks = pl.pallas_call(
        deal_kernel,
        out_shape=jax.ShapeDtypeStruct((LEVELS * CORES * WIDTH, features // 2, quarter), BF16),
        in_specs=[HBM] * 2,
        out_specs=LOCAL,
        scratch_shapes=[
            pltpu.VMEM((CORES, features, rows), BF16),
            pltpu.SemaphoreType.DMA((CORES,)),
        ],
        compiler_params=pltpu.CompilerParams(vmem_limit_bytes=60 << 20),
    )(image, text)
    dealt = lax.all_to_all(chunks, ("level", "core", "width"), 0, 0)

    params = pltpu.CompilerParams(vmem_limit_bytes=6 << 20)
    first = lax.axis_index("core") == 0
    noted = jnp.broadcast_to(matches.astype(BF16), (MARKS, rows))
    other = swap_cores(jnp.concatenate([jnp.where(first, image, text), noted], 0))
    spread, marks = pl.pallas_call(
        spread_kernel,
        out_shape=[
            jax.ShapeDtypeStruct((WIDTH, features, span), BF16),
            jax.ShapeDtypeStruct((MARKS, span), F32),
        ],
        in_specs=[LOCAL] * 3,
        out_specs=[LOCAL] * 2,
        compiler_params=params,
    )(jnp.where(first, text, image), matches, other)
    dealt, spread = lax.optimization_barrier((dealt, spread))
    own, pair = pl.pallas_call(
        gather_kernel,
        out_shape=[piece] * 2,
        in_specs=[LOCAL],
        out_specs=[LOCAL] * 2,
        compiler_params=params,
    )(dealt)

    held = lax.all_to_all(spread, "width", 0, 0)
    held = held.reshape(whole, span)
    far = lax.ppermute(pair, ("row", "level"), far_route(lax.axis_size("row")))
    l1, l2, l3 = (along_line(own, d) for d in (1, 2, 3))

    s1, s2, s3 = pl.pallas_call(
        halo_kernel,
        out_shape=[piece] * 3,
        in_specs=[LOCAL] * 2,
        out_specs=[LOCAL] * 3,
        compiler_params=params,
        cost_estimate=pl.CostEstimate(flops=15 * 10**9, bytes_accessed=2 << 20, transcendentals=0),
    )(pair, far)
    h1, h2, h3 = along_line(s1, 1), along_line(s2, 2), along_line(s3, 3)

    cost = pl.CostEstimate(
        flops=2 * whole * PIECES * quarter * span, bytes_accessed=5 << 20, transcendentals=0
    )
    params = pltpu.CompilerParams(vmem_limit_bytes=12 << 20)
    near = pl.pallas_call(
        near_kernel,
        out_shape=jax.ShapeDtypeStruct((whole, span), F32),
        in_specs=[SMEM, SMEM] + [LOCAL] * 8,
        out_specs=LOCAL,
        compiler_params=params,
        cost_estimate=cost,
    )(scale, shift_bias, marks, own, pair, far, l2, l3, l1, held)
    partial = pl.pallas_call(
        far_kernel,
        out_shape=jax.ShapeDtypeStruct((CORES * WIDTH, features, rows), BF16),
        in_specs=[SMEM, SMEM] + [LOCAL] * 5,
        out_specs=LOCAL,
        compiler_params=params,
        cost_estimate=cost,
    )(scale, shift_bias, h2, h1, h3, held, near)
    terms = lax.all_to_all(partial, ("core", "width"), 0, 0).astype(F32)
    grad_text = terms[0] + terms[1] + terms[2] + terms[3]
    grad_image = terms[4] + terms[5] + terms[6] + terms[7]
    return (scale[0] * grad_image).T, (scale[0] * grad_text).T


def solution(mesh):
    deep = mesh.shape["tour"] // (LEVELS * LINE * CORES)
    fine = Mesh(
        mesh.devices.reshape(deep, LEVELS, LINE, CORES, WIDTH),
        ("row", "level", "x", "core", "width"),
    )
    rows, split = ("row", "level", "x", "core"), "width"
    return jax.shard_map(
        per_device,
        mesh=fine,
        in_specs=(P(rows, split), P(rows, split), P(rows, None), P(), P()),
        out_specs=(P(rows, split), P(rows, split)),
        check_vma=False,
    )
```

```python
import jax
import jax.numpy as jnp
from jax import lax
from jax.experimental import pallas as pl
from jax.experimental.pallas import tpu as pltpu
from jax.sharding import Mesh, PartitionSpec as P

CORES = 2
WIDTH = 4
LEVELS = 2
LINE = 4
BF16 = jnp.bfloat16
F32 = jnp.float32
SMEM = pl.BlockSpec(memory_space=pltpu.SMEM)
LOCAL = pl.BlockSpec(memory_space=pltpu.VMEM)
HBM = pl.BlockSpec(memory_space=pl.ANY)
PIECES = 2 * LINE
MARKS = 16


def swap_cores(block):
    return lax.ppermute(block, "core", [(0, 1), (1, 0)])


def along_line(block, turn):
    return lax.ppermute(block, "x", [((i + turn) % LINE, i) for i in range(LINE)])


def far_route(rows):
    route = []
    for i in range(rows):
        route += [(2 * i, 2 * ((i + 1) % rows)), (2 * i + 1, 2 * ((i - 1) % rows) + 1)]
    return route


def deal_kernel(image, text, chunks, held, sems):
    features, rows = image.shape
    n, half = rows // WIDTH, features // 2
    copies = [
        pltpu.make_async_copy(source, held.at[i], sems.at[i])
        for i, source in enumerate((image, text))
    ]
    for copy in copies:
        copy.start()
    for core in range(CORES):
        copies[core].wait()
        for w in range(WIDTH):
            part = held[core, :, w * n : (w + 1) * n]
            part = jnp.concatenate([part[:half], part[half:]], 1)
            for level in range(LEVELS):
                chunks[(level * CORES + core) * WIDTH + w] = part


def gather_kernel(dealt, own, pair):
    half, n = dealt.shape[1], dealt.shape[2] // 2
    level = lax.axis_index("level")
    for out, at in ((own, level), (pair, 1 - level)):
        for w in range(WIDTH):
            left = dealt[at * CORES * WIDTH + w]
            right = dealt[(at * CORES + 1) * WIDTH + w]
            out[2 * w * half : (2 * w + 1) * half] = jnp.concatenate([left[:, :n], right[:, :n]], 1)
            out[(2 * w + 1) * half : (2 * w + 2) * half] = jnp.concatenate(
                [left[:, n:], right[:, n:]], 1
            )


def spread_kernel(mine, matches, other, spread, marks):
    features, rows = mine.shape
    first = lax.axis_index("core") == 0
    own, others = mine[...], other[:features, :]
    full = (jnp.where(first, own, others), jnp.where(first, others, own))
    for i in range(WIDTH):
        spread[i, :, :rows] = full[0]
        spread[i, :, rows:] = full[1]
    own_marks = jnp.broadcast_to(matches[...].astype(F32), (MARKS, rows))
    other_marks = other[features:, :].astype(F32)
    marks[:, :rows] = jnp.where(first, own_marks, other_marks)
    marks[:, rows:] = jnp.where(first, other_marks, own_marks)


def weighed(pieces, held, scale, bias):
    logits = lax.dot_general(
        pieces, held[...], (((0,), (0,)), ((), ())), preferred_element_type=F32
    )
    return jax.nn.sigmoid(scale[0] * logits + bias[0])


def halo_kernel(pair, far, *outs):
    x, level = lax.axis_index("x"), lax.axis_index("level")
    for turn, out in enumerate(outs, 1):
        higher = lax.rem(x + LINE - turn, LINE) > x
        out[...] = jnp.where(higher == (level == 0), pair[...], far[...])


def label_of(marks, n):
    span = marks.shape[1]
    rows = span // CORES
    first, w = lax.axis_index("core") == 0, lax.axis_index("width")
    down = lax.broadcasted_iota(jnp.int32, (n, 1), 0)
    lane = lax.broadcasted_iota(jnp.int32, (1, span), 1)
    part = n // CORES
    block, row = down // part, w * part + down % part
    mark = jnp.where(lane == block * rows + row, marks[0:1, :], 0.0)
    have = jnp.where(first, jnp.sum(mark, axis=1, keepdims=True), row.astype(F32))
    goal = jnp.where(first, (lane % rows).astype(F32), marks[0:1, :])
    return ((have == goal) & (lane // rows == block)).astype(F32)


def near_kernel(scale, bias, marks, own, l2, l3, l1, held, out):
    n = l1.shape[1]
    pieces = jnp.concatenate([own[...], l1[...], l2[...], l3[...]], 1)
    probs = weighed(pieces, held, scale, bias)
    weights = jnp.concatenate([(probs[:n] - label_of(marks, n)).astype(BF16), probs[n:].astype(BF16)], 0)
    out[...] = jnp.dot(pieces, weights, preferred_element_type=F32)


def far_kernel(scale, bias, pair, far, h2, h1, h3, held, near, out):
    whole, n = h1.shape
    span = held.shape[1]
    rows = span // CORES
    features = whole // WIDTH
    level = lax.axis_index("level")
    side = lax.broadcasted_iota(jnp.int32, (whole, n), 1) < n // CORES
    last = jnp.where(side == (level == 0), pair[...], far[...])
    pieces = jnp.concatenate([last, h1[...], h2[...], h3[...]], 1)
    probs = weighed(pieces, held, scale, bias)
    lane = lax.broadcasted_iota(jnp.int32, (n, span), 1)
    down = lax.broadcasted_iota(jnp.int32, (n, span), 0)
    met = lane // rows != down // (n // CORES)
    weights = jnp.concatenate(
        [
            jnp.where(met, probs[:n], 0.0).astype(BF16),
            probs[n:].astype(BF16),
        ],
        0,
    )
    for to in range(WIDTH):
        at = slice(to * features, (to + 1) * features)
        total = near[at, :] + jnp.dot(pieces[at], weights, preferred_element_type=F32)
        total = total.astype(BF16)
        for core in range(CORES):
            out[core * WIDTH + to] = total[:, core * rows : (core + 1) * rows]


def per_device(images, texts, matches, scale, shift_bias):
    features, rows = images.shape[1], images.shape[0]
    span = CORES * rows
    quarter = span // WIDTH
    whole = WIDTH * features

    image, text = images.T, texts.T
    piece = jax.ShapeDtypeStruct((whole, quarter), BF16)
    chunks = pl.pallas_call(
        deal_kernel,
        out_shape=jax.ShapeDtypeStruct((LEVELS * CORES * WIDTH, features // 2, quarter), BF16),
        in_specs=[HBM] * 2,
        out_specs=LOCAL,
        scratch_shapes=[
            pltpu.VMEM((CORES, features, rows), BF16),
            pltpu.SemaphoreType.DMA((CORES,)),
        ],
        compiler_params=pltpu.CompilerParams(vmem_limit_bytes=60 << 20),
    )(image, text)
    dealt = lax.all_to_all(chunks, ("level", "core", "width"), 0, 0)

    params = pltpu.CompilerParams(vmem_limit_bytes=4 << 20)
    first = lax.axis_index("core") == 0
    noted = jnp.broadcast_to(matches.astype(BF16), (MARKS, rows))
    other = swap_cores(jnp.concatenate([jnp.where(first, image, text), noted], 0))
    spread, marks = pl.pallas_call(
        spread_kernel,
        out_shape=[
            jax.ShapeDtypeStruct((WIDTH, features, span), BF16),
            jax.ShapeDtypeStruct((MARKS, span), F32),
        ],
        in_specs=[LOCAL] * 3,
        out_specs=[LOCAL] * 2,
        compiler_params=params,
    )(jnp.where(first, text, image), matches, other)
    dealt, spread = lax.optimization_barrier((dealt, spread))
    own, pair = pl.pallas_call(
        gather_kernel,
        out_shape=[piece] * 2,
        in_specs=[LOCAL],
        out_specs=[LOCAL] * 2,
        compiler_params=params,
    )(dealt)

    held = lax.all_to_all(spread, "width", 0, 0)
    held = held.reshape(whole, span)
    far = lax.ppermute(pair, ("row", "level"), far_route(lax.axis_size("row")))
    l1, l2, l3 = (along_line(own, d) for d in (1, 2, 3))

    s1, s2, s3 = pl.pallas_call(
        halo_kernel,
        out_shape=[piece] * 3,
        in_specs=[LOCAL] * 2,
        out_specs=[LOCAL] * 3,
        compiler_params=params,
        cost_estimate=pl.CostEstimate(flops=15 * 10**9, bytes_accessed=2 << 20, transcendentals=0),
    )(pair, far)
    h1, h2, h3 = along_line(s1, 1), along_line(s2, 2), along_line(s3, 3)

    cost = pl.CostEstimate(
        flops=2 * whole * PIECES * quarter * span, bytes_accessed=5 << 20, transcendentals=0
    )
    params = pltpu.CompilerParams(vmem_limit_bytes=4 << 20)
    near = pl.pallas_call(
        near_kernel,
        out_shape=jax.ShapeDtypeStruct((whole, span), F32),
        in_specs=[SMEM, SMEM] + [LOCAL] * 6,
        out_specs=LOCAL,
        compiler_params=params,
        cost_estimate=cost,
    )(scale, shift_bias, marks, own, l2, l3, l1, held)
    partial = pl.pallas_call(
        far_kernel,
        out_shape=jax.ShapeDtypeStruct((CORES * WIDTH, features, rows), BF16),
        in_specs=[SMEM, SMEM] + [LOCAL] * 7,
        out_specs=LOCAL,
        compiler_params=params,
        cost_estimate=cost,
    )(scale, shift_bias, pair, far, h2, h1, h3, held, near)
    terms = lax.all_to_all(partial, ("core", "width"), 0, 0).astype(F32)
    grad_text = terms[0] + terms[1] + terms[2] + terms[3]
    grad_image = terms[4] + terms[5] + terms[6] + terms[7]
    return (scale[0] * grad_image).T, (scale[0] * grad_text).T


def solution(mesh):
    deep = mesh.shape["tour"] // (LEVELS * LINE * CORES)
    fine = Mesh(
        mesh.devices.reshape(deep, LEVELS, LINE, CORES, WIDTH),
        ("row", "level", "x", "core", "width"),
    )
    rows, split = ("row", "level", "x", "core"), "width"
    return jax.shard_map(
        per_device,
        mesh=fine,
        in_specs=(P(rows, split), P(rows, split), P(rows, None), P(), P()),
        out_specs=(P(rows, split), P(rows, split)),
        check_vma=False,
    )
```
